32 devices in a mesh: dp: 8 (over z, y), tensor: 4 (over x, core).
Axes of the slice: x: 2, y: 2, z: 4, core: 2. Of those that a mesh axis runs over, the one named last changes fastest.
Arguments:
- inputs: bfloat16 [32, 197, 768], P(('dp', 'tensor')), may hold values from -6 to 6
- ln1_gain: bfloat16 [768], P('dp'), may hold values from 0.5 to 1.5
- ln1_bias: bfloat16 [768], P('dp'), may hold values from -3 to 3
- qkv_weight: bfloat16 [768, 3, 768], P('dp', None, 'tensor'), may hold values from -0.21875 to 0.21875
- proj_weight: bfloat16 [768, 768], P('tensor', 'dp'), may hold values from -1.5 to 1.5
- proj_bias: bfloat16 [768], P('dp'), may hold values from -1.5 to 1.5
- ln2_gain: bfloat16 [768], P('dp'), may hold values from 0.5 to 1.5
- ln2_bias: bfloat16 [768], P('dp'), may hold values from -3 to 3
- router_weight: bfloat16 [768, 4], P('dp'), may hold values from -0.15625 to 0.15625
- expert_in: bfloat16 [4, 768, 3072], P(None, 'dp', 'tensor'), may hold values from -0.21875 to 0.21875
- expert_in_bias: bfloat16 [4, 3072], P(None, 'tensor'), may hold values from -1.5 to 1.5
- expert_out: bfloat16 [4, 3072, 768], P(None, 'tensor', 'dp'), may hold values from -0.4375 to 0.4375
- expert_out_bias: bfloat16 [4, 768], P(None, 'dp'), may hold values from -4 to 4
- expert_ids: int32 [32, 197, 2], P('dp'), may hold values from 0 to 3, as said below
- slot_ids: int32 [32, 197, 2], P('dp'), may hold values from 0 to 414, as said below
- cotangent: bfloat16 [32, 197, 768], P(('dp', 'tensor')), may hold values from -6 to 6
Outputs:
- block_out: bfloat16 [32, 197, 768], P(('dp', 'tensor'))
- input_grad: float32 [32, 197, 768], P(('dp', 'tensor'))
- ln1_gain_grad: float32 [768], P('dp')
- ln1_bias_grad: float32 [768], P('dp')
- qkv_weight_grad: float32 [768, 3, 768], P('dp', None, 'tensor')
- proj_weight_grad: float32 [768, 768], P('tensor', 'dp')
- proj_bias_grad: float32 [768], P('dp')
- ln2_gain_grad: float32 [768], P('dp')
- ln2_bias_grad: float32 [768], P('dp')
- router_grad: float32 [768, 4], P('dp')
- expert_in_grad: float32 [4, 768, 3072], P(None, 'dp', 'tensor')
- expert_in_bias_grad: float32 [4, 3072], P(None, ('dp', 'tensor'))
- expert_out_grad: float32 [4, 3072, 768], P(None, 'tensor', 'dp')
- expert_out_bias_grad: float32 [4, 768], P(None, 'dp')
The draws below stay inside these ranges and needn't reach their ends.
Inputs may be any that keep to these rules, and one draw needn't show every extreme that they name: `expert_ids`: the two experts of a token differ. Within one group of 4 images (one index of dp) every pair of expert and slot is used at most once, an expert's used slots are 0 up to its count less one, and one expert uses all 415 slots. `slot_ids`: the slot that goes with expert_ids of the same entry.
All inputs are finite; a program needn't handle non-finite values.
Results may differ from the reference program's by a relative error of at most 0.013.
Values may be sent and summed in bfloat16 or wider, within the bound.
A program may use at most 128 MiB of HBM per device.

```python
import math
import jax
import jax.numpy as jnp
from jax import lax

D = 768
HEADS = 12
HEAD_DIM = 64
FF = 3072
SEQ = 197
EXPERTS = 4
IMG_DEV = 4
IMAGES = 32
CAP = 415


def route_tables(key):
    key = jax.random.fold_in(key, 101)
    groups = IMAGES // IMG_DEV
    tokens = IMG_DEV * SEQ
    spare_slots = EXPERTS * CAP - 2 * tokens

    def one_group(group_key):
        cut_key, order_key, token_key, swap_key = jax.random.split(group_key, 4)
        cut_points = jnp.sort(jax.random.randint(cut_key, (EXPERTS - 2,), 0, spare_slots + 1))
        boundaries = jnp.concatenate([jnp.zeros((1,), jnp.int32), cut_points.astype(jnp.int32), jnp.full((1,), spare_slots, jnp.int32)])
        shortfall = jnp.concatenate([jnp.zeros((1,), jnp.int32), boundaries[1:] - boundaries[:-1]])
        expert_loads = CAP - shortfall
        starts = jnp.cumsum(expert_loads) - expert_loads
        finishes = starts + expert_loads
        positions = jnp.arange(2 * tokens, dtype=jnp.int32)
        rank_of = jnp.sum((positions[:, None] >= finishes[None, :]).astype(jnp.int32), axis=1)
        expert_order = jax.random.permutation(order_key, EXPERTS).astype(jnp.int32)
        experts_at = expert_order[rank_of]
        slots_at = positions - starts[rank_of]
        shuffle = jax.random.permutation(token_key, tokens)
        pair_experts = jnp.stack([experts_at[:tokens], experts_at[tokens:]], axis=1)[shuffle]
        pair_slots = jnp.stack([slots_at[:tokens], slots_at[tokens:]], axis=1)[shuffle]
        swapped = jax.random.randint(swap_key, (tokens, 1), 0, 2)
        pair_experts = jnp.where(swapped == 1, pair_experts[:, ::-1], pair_experts)
        pair_slots = jnp.where(swapped == 1, pair_slots[:, ::-1], pair_slots)
        return (pair_experts.reshape(IMG_DEV, SEQ, 2), pair_slots.reshape(IMG_DEV, SEQ, 2))
    tables = jax.vmap(one_group)(jax.random.split(key, groups))
    return (tables[0].reshape(IMAGES, SEQ, 2).astype(jnp.int32), tables[1].reshape(IMAGES, SEQ, 2).astype(jnp.int32))


def draw_expert_ids(key, part):
    return route_tables(key)[0]


def draw_slot_ids(key, part):
    return route_tables(key)[1]


def steps_of(stream_key, shape, cuts, least, largest):
    loudness, own = 1.0, jax.random.fold_in(stream_key, 6)
    for dim, parts in cuts:
        heights = jnp.exp(jax.random.uniform(jax.random.fold_in(own, dim), (parts,), jnp.float32, least / len(cuts), largest / len(cuts)))
        loudness = loudness * jnp.repeat(heights, shape[dim] // parts).reshape([-1 if axis == dim else 1 for axis in range(len(shape))])
    return loudness


def scatter_about(own_key, extent, scale, bound, pieces=(), held_as=jnp.bfloat16):
    factor_of = steps_of(own_key, extent, pieces, -0.22, 0.18) if pieces else 1.0
    drawn = jax.random.normal(own_key, extent, jnp.float32) * scale * factor_of
    return jnp.minimum(jnp.maximum(drawn, -bound), bound).astype(held_as)


def setup_inputs(seed: int = 0) -> dict:
    keys = jax.random.split(jax.random.key(seed), 17)
    inputs = scatter_about(keys[0], (IMAGES, SEQ, D), 1.0, 6.0, ((0, 32),))
    ln1_gain = jnp.clip(1.0 + 0.1 * jax.random.normal(keys[1], (D,), jnp.float32), 0.5, 1.5).astype(jnp.bfloat16)
    ln1_bias = scatter_about(keys[2], (D,), 0.2, 3.0, ((0, 8),))
    qkv_weight = scatter_about(keys[3], (D, 3, D), D ** -0.5, 0.21875, ((0, 8), (2, 4)))
    proj_weight = scatter_about(keys[4], (D, D), (D * 4 // SEQ) ** -0.5, 1.5, ((0, 4), (1, 8)))
    proj_bias = scatter_about(keys[5], (D,), 0.1, 1.5, ((0, 8),))
    ln2_gain = jnp.clip(1.0 + 0.1 * jax.random.normal(keys[6], (D,), jnp.float32), 0.5, 1.5).astype(jnp.bfloat16)
    ln2_bias = scatter_about(keys[7], (D,), 0.2, 3.0, ((0, 8),))
    router_weight = scatter_about(keys[8], (D, EXPERTS), (2 * D) ** -0.5, 0.15625, ((0, 8),))
    expert_in = scatter_about(keys[9], (EXPERTS, D, FF), D ** -0.5, 0.21875, ((1, 8), (2, 4)))
    expert_in_bias = scatter_about(keys[10], (EXPERTS, FF), 0.1, 1.5, ((1, 4),))
    expert_out = scatter_about(keys[11], (EXPERTS, FF, D), (FF // 16) ** -0.5, 0.4375, ((1, 4), (2, 8)))
    expert_out_bias = scatter_about(keys[12], (EXPERTS, D), 0.25, 4.0, ((1, 8),))
    expert_ids = draw_expert_ids(jax.random.fold_in(keys[16], 71), 0)
    slot_ids = draw_slot_ids(jax.random.fold_in(keys[16], 71), 0)
    cotangent = scatter_about(keys[15], (IMAGES, SEQ, D), 1.0, 6.0, ((0, 32),))
    return {"inputs": inputs, "ln1_gain": ln1_gain, "ln1_bias": ln1_bias, "qkv_weight": qkv_weight, "proj_weight": proj_weight, "proj_bias": proj_bias, "ln2_gain": ln2_gain, "ln2_bias": ln2_bias, "router_weight": router_weight, "expert_in": expert_in, "expert_in_bias": expert_in_bias, "expert_out": expert_out, "expert_out_bias": expert_out_bias, "expert_ids": expert_ids, "slot_ids": slot_ids, "cotangent": cotangent}


EPSILON = 1e-06
PRECISE = lax.Precision.HIGHEST

@jax.custom_vjp
def low(v):
    return lax.optimization_barrier(v.astype(jnp.bfloat16)).astype(jnp.float32)

@jax.custom_vjp
def low_back(v):
    return v

def low_keep(v):
    return (low(v), None)

def low_pass(kept, grad):
    return (grad,)

def back_keep(v):
    return (v, None)

def back_low(kept, grad):
    return (low(grad),)
low.defvjp(low_keep, low_pass)
low_back.defvjp(back_keep, back_low)

def layer_norm(values, gain, bias):
    centred = values - lax.optimization_barrier(jnp.mean(values, axis=-1, keepdims=True))
    spread = lax.optimization_barrier(jnp.mean(centred * centred, axis=-1, keepdims=True))
    return centred * lax.rsqrt(spread + EPSILON) * gain + bias

def group_forward(params, source, choice_ids, slot_table):
    gain_one, bias_one, qkv_weight, proj_weight, proj_bias, gain_two, bias_two, router_weight, expert_in, expert_in_bias, expert_out, expert_out_bias = params
    images = source.shape[0]
    tokens = images * SEQ
    score_scale = 1.0 / math.sqrt(HEAD_DIM)
    normed_one = low(layer_norm(source, gain_one, bias_one))
    mixed = jnp.einsum('bsd,dkf->bskf', normed_one, qkv_weight, precision=PRECISE)
    mixed = mixed.reshape(images, SEQ, 3, HEADS, HEAD_DIM)
    queries = low(low_back(mixed[:, :, 0]))
    keys_all = low(low_back(mixed[:, :, 1]))
    values_all = low(low_back(mixed[:, :, 2]))
    scores = low_back(jnp.einsum('bqhe,bkhe->bhqk', queries, keys_all, precision=PRECISE) * score_scale)
    weights = low(jax.nn.softmax(scores, axis=-1))
    attended = low(low_back(jnp.einsum('bhqk,bkhe->bqhe', weights, values_all, precision=PRECISE)))
    attended = attended.reshape(images, SEQ, HEADS * HEAD_DIM)
    branch = low_back(jnp.einsum('bsf,fd->bsd', attended, proj_weight, precision=PRECISE))
    state = source + branch + proj_bias
    normed_two = low(layer_norm(state, gain_two, bias_two))
    rows = normed_two.reshape(tokens, D)
    router_probs = jax.nn.softmax(jnp.dot(rows, router_weight, precision=PRECISE), axis=-1)
    gate_values = jnp.take_along_axis(router_probs, choice_ids, axis=1)
    places = (choice_ids * CAP + slot_table).reshape(2 * tokens).astype(jnp.int32)
    dispatched = jnp.zeros((EXPERTS * CAP, D), jnp.float32).at[places].add(jnp.repeat(rows, 2, axis=0))
    dispatched = dispatched.reshape(EXPERTS, CAP, D)
    pre = low_back(jnp.einsum('ecd,edf->ecf', dispatched, expert_in, precision=PRECISE) + expert_in_bias[:, None, :])
    hidden = low(jax.nn.gelu(pre, approximate=True))
    results = low_back(jnp.einsum('ecf,efd->ecd', hidden, expert_out, precision=PRECISE)).reshape(EXPERTS * CAP, D)
    picked = results[places].reshape(tokens, 2, D) + expert_out_bias[choice_ids]
    mixed_out = lax.optimization_barrier(jnp.sum(gate_values[:, :, None] * picked, axis=1))
    return state + mixed_out.reshape(images, SEQ, D)

def reference(inputs, ln1_gain, ln1_bias, qkv_weight, proj_weight, proj_bias, ln2_gain, ln2_bias, router_weight, expert_in, expert_in_bias, expert_out, expert_out_bias, expert_ids, slot_ids, cotangent):
    params = (ln1_gain.astype(jnp.float32), ln1_bias.astype(jnp.float32), qkv_weight.astype(jnp.float32), proj_weight.astype(jnp.float32), proj_bias.astype(jnp.float32), ln2_gain.astype(jnp.float32), ln2_bias.astype(jnp.float32), router_weight.astype(jnp.float32), expert_in.astype(jnp.float32), expert_in_bias.astype(jnp.float32), expert_out.astype(jnp.float32), expert_out_bias.astype(jnp.float32))
    groups = inputs.shape[0] // IMG_DEV
    source = inputs.astype(jnp.float32).reshape(groups, IMG_DEV, SEQ, D)
    choice_ids = expert_ids.reshape(groups, IMG_DEV * SEQ, 2).astype(jnp.int32)
    slot_table = slot_ids.reshape(groups, IMG_DEV * SEQ, 2).astype(jnp.int32)

    def whole(params_in, source_in):

        def run_group(bundle):
            return group_forward(params_in, bundle[0], bundle[1], bundle[2])
        return lax.map(jax.checkpoint(run_group), (source_in, choice_ids, slot_table))
    result, pullback = jax.vjp(whole, params, source)
    seeds = cotangent.astype(jnp.float32).reshape(result.shape)
    grads, source_grad = pullback(seeds)
    block_out = result.reshape(inputs.shape[0], SEQ, D).astype(jnp.bfloat16)
    input_grad = source_grad.reshape(inputs.shape[0], SEQ, D)
    return (block_out, input_grad, grads[0], grads[1], grads[2], grads[3], grads[4], grads[5], grads[6], grads[7], grads[8], grads[9], grads[10], grads[11])
```

```python
import jax
import jax.numpy as jnp
from jax import lax
from jax.sharding import PartitionSpec as P

HEAD_DIM = 64
SEQ = 197


EPSILON = 1e-06
PRECISE = lax.Precision.HIGHEST


def layer_norm(values, gain, bias):
    centred = values - jnp.mean(values, axis=-1, keepdims=True)
    spread = jnp.mean(centred * centred, axis=-1, keepdims=True)
    return centred * lax.rsqrt(spread + EPSILON) * gain + bias


def gelu_tanh(values):
    return jax.nn.gelu(values, approximate=True)


def per_device(
    inputs,
    ln1_gain,
    ln1_bias,
    qkv_weight,
    proj_weight,
    proj_bias,
    ln2_gain,
    ln2_bias,
    router_weight,
    expert_in,
    expert_in_bias,
    expert_out,
    expert_out_bias,
    expert_ids,
    slot_ids,
    cotangent,
):
    local_images, seq_len, model_width = inputs.shape
    tensor_count = lax.axis_size("tensor")
    dp_count = lax.axis_size("dp")
    tensor_rank = lax.axis_index("tensor")
    dp_rank = lax.axis_index("dp")
    group_images = local_images * tensor_count
    experts = expert_in.shape[0]
    tokens = group_images * SEQ
    slot_count = 40 * tokens // (19 * experts) + 1
    slot_rows = -(-slot_count // 16) * 16
    heads_local = qkv_weight.shape[2] // HEAD_DIM
    score_scale = HEAD_DIM ** (-0.5)

    def own_rows(values):
        return lax.dynamic_slice_in_dim(values, tensor_rank * local_images, local_images, 0)

    def scatter_rows(values):
        return lax.psum_scatter(
            values.astype(jnp.bfloat16), "tensor", scatter_dimension=0, tiled=True
        ).astype(jnp.float32)

    def split_three(values):
        first = values.astype(jnp.bfloat16)
        rest = values - first.astype(jnp.float32)
        second = rest.astype(jnp.bfloat16)
        third = (rest - second.astype(jnp.float32)).astype(jnp.bfloat16)
        return jnp.concatenate([first, second, third], axis=-1)

    def fetch_attention():
        return (
            lax.all_gather(qkv_weight, "dp", axis=0, tiled=True),
            lax.all_gather(proj_weight, "dp", axis=1, tiled=True),
            lax.all_gather(ln1_gain, "dp", axis=0, tiled=True),
            lax.all_gather(ln1_bias, "dp", axis=0, tiled=True),
            lax.all_gather(proj_bias, "dp", axis=0, tiled=True),
        )

    def fetch_experts():
        return (
            lax.all_gather(expert_in, "dp", axis=1, tiled=True),
            lax.all_gather(expert_out, "dp", axis=2, tiled=True),
            lax.all_gather(router_weight, "dp", axis=0, tiled=True),
            lax.all_gather(expert_out_bias, "dp", axis=1, tiled=True),
            lax.all_gather(ln2_gain, "dp", axis=0, tiled=True),
            lax.all_gather(ln2_bias, "dp", axis=0, tiled=True),
        )

    def scores_of(query_heads, key_heads):
        return (
            jnp.einsum(
                "bqhe,bkhe->bhqk", query_heads, key_heads, preferred_element_type=jnp.float32
            )
            * score_scale
        )

    qkv_full, proj_full, gain_one, bias_one, proj_shift = fetch_attention()
    gain_one_f = gain_one.astype(jnp.float32)
    bias_one_f = bias_one.astype(jnp.float32)
    source = inputs.astype(jnp.float32)
    normed_one = layer_norm(source, gain_one_f, bias_one_f).astype(jnp.bfloat16)
    rows_one = lax.all_gather(normed_one, "tensor", axis=0, tiled=True)
    mixed = jnp.einsum(
        "bsd,dkf->bskf", rows_one, qkv_full, preferred_element_type=jnp.float32
    ).astype(jnp.bfloat16)
    head_blocks = mixed.reshape(group_images, seq_len, 3, heads_local, HEAD_DIM)
    query_heads = head_blocks[:, :, 0]
    key_heads = head_blocks[:, :, 1]
    value_heads = head_blocks[:, :, 2]
    scores = scores_of(query_heads, key_heads)
    top_score = jnp.max(scores, axis=-1, keepdims=True)
    raised = jnp.exp(scores - top_score)
    row_total = jnp.sum(raised, axis=-1, keepdims=True)
    weights = raised / row_total
    log_total = top_score + jnp.log(row_total)
    attended = jnp.einsum(
        "bhqk,bkhe->bqhe",
        weights.astype(jnp.bfloat16),
        value_heads,
        preferred_element_type=jnp.float32,
    )
    attended = attended.astype(jnp.bfloat16).reshape(group_images, seq_len, heads_local * HEAD_DIM)
    attn_terms = jnp.einsum("bsf,fd->bsd", attended, proj_full, preferred_element_type=jnp.float32)
    attn_sum = scatter_rows(attn_terms)
    state = source + attn_sum + proj_shift.astype(jnp.float32)
    in_full, out_full, router_full, back_shift, gain_two, bias_two = fetch_experts()
    gain_two_f = gain_two.astype(jnp.float32)
    bias_two_f = bias_two.astype(jnp.float32)
    normed_two = layer_norm(state, gain_two_f, bias_two_f).astype(jnp.bfloat16)
    rows_two = lax.all_gather(normed_two, "tensor", axis=0, tiled=True)
    out_rows = lax.all_gather(cotangent, "tensor", axis=0, tiled=True)
    token_rows = rows_two.reshape(tokens, model_width)
    grad_rows = out_rows.reshape(tokens, model_width)
    choice_ids = expert_ids.reshape(tokens, 2)
    places = choice_ids * slot_rows + slot_ids.reshape(tokens, 2)
    slot_index = jnp.arange(experts * slot_rows, dtype=jnp.int32)[:, None]
    chosen = (
        (slot_index == places[:, 0][None, :]) | (slot_index == places[:, 1][None, :])
    ).astype(jnp.bfloat16)
    logits = jnp.dot(token_rows, router_full, preferred_element_type=jnp.float32)
    router_probs = jax.nn.softmax(logits, axis=-1)
    expert_mask = (
        jnp.arange(experts * slot_rows)[:, None] // slot_rows == jnp.arange(experts)[None, :]
    )
    slot_probs = jnp.dot(chosen, split_three(router_probs), preferred_element_type=jnp.float32)
    slot_gates = jnp.sum(
        jnp.where(expert_mask[:, None, :], slot_probs.reshape(-1, 3, experts), 0.0), axis=(1, 2)
    )
    dispatched = (
        jnp.dot(chosen, token_rows, preferred_element_type=jnp.float32)
        .astype(jnp.bfloat16)
        .reshape(experts, slot_rows, model_width)
    )
    slot_out = (
        jnp.dot(chosen, grad_rows, preferred_element_type=jnp.float32)
    )
    slot_grad = (
        (slot_gates[:, None] * slot_out)
        .astype(jnp.bfloat16)
        .reshape(experts, slot_rows, model_width)
    )
    pre = (
        jnp.einsum("ecd,edf->ecf", dispatched, in_full, preferred_element_type=jnp.float32)
        + expert_in_bias.astype(jnp.float32)[:, None, :]
    )
    hidden = gelu_tanh(pre).astype(jnp.bfloat16)
    expert_terms = jnp.einsum(
        "ecf,efd->ecd", hidden, out_full, preferred_element_type=jnp.float32
    ).reshape(experts * slot_rows, model_width)
    gated_terms = (slot_gates[:, None] * expert_terms).astype(jnp.bfloat16)
    slot_dgate = jnp.sum(expert_terms * slot_out, axis=-1)
    mixed_terms = jnp.einsum(
        "st,sd->td", chosen, gated_terms, preferred_element_type=jnp.float32
    )
    mixed_sum = scatter_rows(mixed_terms.reshape(group_images, seq_len, model_width))
    own_ids = own_rows(expert_ids.reshape(group_images, seq_len, 2))
    onehot_own = (own_ids[..., None] == jnp.arange(experts)).astype(jnp.float32)
    probs_own = own_rows(router_probs.reshape(group_images, seq_len, experts))
    probs_chosen = probs_own * jnp.sum(onehot_own, axis=2)
    back_f = back_shift.astype(jnp.float32)
    shift_own = jnp.einsum("bpe,ed->bpd", probs_chosen, back_f, precision=PRECISE)
    result = state + mixed_sum + shift_own
    block_out = result.astype(jnp.bfloat16)
    own_grad = cotangent.astype(jnp.float32)
    out_grad = jnp.einsum("ecf,ecd->efd", hidden, slot_grad, preferred_element_type=jnp.float32)
    out_part = lax.psum_scatter(
        out_grad.astype(jnp.bfloat16), "dp", scatter_dimension=2, tiled=True
    ).astype(jnp.float32)
    hidden_grad = jnp.einsum(
        "ecd,efd->ecf", slot_grad, out_full, preferred_element_type=jnp.float32
    )
    gelu_pull = jax.vjp(gelu_tanh, pre)[1]
    pre_grad = gelu_pull(hidden_grad)[0].astype(jnp.bfloat16)
    in_grad = jnp.einsum("ecd,ecf->edf", dispatched, pre_grad, preferred_element_type=jnp.float32)
    in_bias_grad = jnp.sum(pre_grad.astype(jnp.float32), axis=1)
    in_part = lax.psum_scatter(
        in_grad.astype(jnp.bfloat16), "dp", scatter_dimension=1, tiled=True
    ).astype(jnp.float32)
    slot_back = (
        jnp.einsum("ecf,edf->ecd", pre_grad, in_full, preferred_element_type=jnp.float32)
        .astype(jnp.bfloat16)
        .reshape(experts * slot_rows, model_width)
    )
    row_back = jnp.einsum("st,sd->td", chosen, slot_back, preferred_element_type=jnp.float32)
    dgate_cols = split_three(jnp.where(expert_mask, slot_dgate[:, None], 0.0))
    prob_parts = jnp.sum(
        jnp.einsum("st,sk->tk", chosen, dgate_cols, preferred_element_type=jnp.float32).reshape(
            tokens, 3, experts
        ),
        axis=1,
    )
    row_sum = scatter_rows(row_back.reshape(group_images, seq_len, model_width))
    prob_sum = lax.psum_scatter(
        prob_parts.reshape(group_images, seq_len, experts),
        "tensor",
        scatter_dimension=0,
        tiled=True,
    )
    prob_grad = prob_sum + jnp.sum(onehot_own, axis=2) * jnp.einsum(
        "bpd,ed->bpe", own_grad, back_f, precision=PRECISE
    )
    logit_grad = probs_own * (prob_grad - jnp.sum(probs_own * prob_grad, axis=-1, keepdims=True))
    normed_grad = row_sum + jnp.einsum(
        "bpe,de->bpd", logit_grad, router_full.astype(jnp.float32), precision=PRECISE
    )
    router_grad = jnp.einsum(
        "bpd,bpe->de", normed_two.astype(jnp.float32), logit_grad, precision=PRECISE
    )
    back_bias_grad = jnp.einsum("bpe,bpd->ed", probs_chosen, own_grad, precision=PRECISE)
    norm_two_pull = jax.vjp(layer_norm, state, gain_two_f, bias_two_f)[1]
    state_grad, gain_two_grad, bias_two_grad = norm_two_pull(normed_grad)
    state_grad = state_grad + own_grad
    proj_bias_grad = jnp.sum(state_grad, axis=(0, 1))
    state_rows = lax.all_gather(state_grad.astype(jnp.bfloat16), "tensor", axis=0, tiled=True)
    proj_grad = jnp.einsum("bsf,bsd->fd", attended, state_rows, preferred_element_type=jnp.float32)
    attended_grad = jnp.einsum(
        "bsd,fd->bsf", state_rows, proj_full, preferred_element_type=jnp.float32
    )
    attended_grad = attended_grad.astype(jnp.bfloat16).reshape(
        group_images, seq_len, heads_local, HEAD_DIM
    )
    weight_grad = jnp.einsum(
        "bqhe,bkhe->bhqk", attended_grad, value_heads, preferred_element_type=jnp.float32
    )
    centre = jnp.sum(weights * weight_grad, axis=-1, keepdims=True)
    score_grad = (weights * (weight_grad - centre)).astype(jnp.bfloat16)
    query_grad = (
        jnp.einsum("bhqk,bkhe->bqhe", score_grad, key_heads, preferred_element_type=jnp.float32)
        * score_scale
    )
    key_grad = (
        jnp.einsum("bhqk,bqhe->bkhe", score_grad, query_heads, preferred_element_type=jnp.float32)
        * score_scale
    )
    value_grad = jnp.einsum(
        "bhqk,bqhe->bkhe",
        weights.astype(jnp.bfloat16),
        attended_grad,
        preferred_element_type=jnp.float32,
    )
    heads_grad = jnp.stack([query_grad, key_grad, value_grad], axis=2).astype(jnp.bfloat16)
    heads_grad = heads_grad.reshape(group_images, seq_len, 3, heads_local * HEAD_DIM)
    qkv_grad = jnp.einsum("bsd,bskf->dkf", rows_one, heads_grad, preferred_element_type=jnp.float32)
    rows_grad = jnp.einsum(
        "bskf,dkf->bsd", heads_grad, qkv_full, preferred_element_type=jnp.float32
    )
    normed_one_grad = scatter_rows(rows_grad)
    norm_one_pull = jax.vjp(layer_norm, source, gain_one_f, bias_one_f)[1]
    source_grad, gain_one_grad, bias_one_grad = norm_one_pull(normed_one_grad)
    input_grad = state_grad + source_grad
    qkv_part = lax.psum_scatter(
        qkv_grad.astype(jnp.bfloat16), "dp", scatter_dimension=0, tiled=True
    ).astype(jnp.float32)
    proj_part = lax.psum_scatter(
        proj_grad.astype(jnp.bfloat16), "dp", scatter_dimension=1, tiled=True
    ).astype(jnp.float32)
    share = model_width // dp_count
    hidden_cols = in_bias_grad.shape[1]
    bias_share = hidden_cols // dp_count
    bias_full = lax.dynamic_update_slice_in_dim(
        jnp.zeros((experts, hidden_cols * tensor_count), jnp.float32),
        in_bias_grad,
        tensor_rank * hidden_cols,
        1,
    )
    packed = jnp.concatenate(
        [
            gain_one_grad.reshape(dp_count, share),
            bias_one_grad.reshape(dp_count, share),
            proj_bias_grad.reshape(dp_count, share),
            gain_two_grad.reshape(dp_count, share),
            bias_two_grad.reshape(dp_count, share),
            router_grad.reshape(dp_count, share * experts),
            back_bias_grad.reshape(experts, dp_count, share).transpose(1, 0, 2).reshape(dp_count, -1),
            bias_full.reshape(experts, dp_count, -1).transpose(1, 0, 2).reshape(dp_count, -1),
        ],
        axis=1,
    )
    totals = lax.psum(
        lax.psum_scatter(packed, "dp", scatter_dimension=0, tiled=True).reshape(-1), "tensor"
    )
    cuts = []
    at = 0
    for width in (share,) * 5 + (share * experts,) * 2:
        cuts.append(totals[at : at + width])
        at += width
    in_bias_out = lax.dynamic_slice_in_dim(
        totals[at:].reshape(experts, tensor_count * bias_share), tensor_rank * bias_share, bias_share, 1
    )
    return (
        block_out,
        input_grad,
        cuts[0],
        cuts[1],
        qkv_part,
        proj_part,
        cuts[2],
        cuts[3],
        cuts[4],
        cuts[5].reshape(share, experts),
        in_part,
        in_bias_out,
        out_part,
        cuts[6].reshape(experts, share),
    )


def solution(mesh):
    placed = (
        P(("dp", "tensor"), None, None),
        P("dp"),
        P("dp"),
        P("dp", None, "tensor"),
        P("tensor", "dp"),
        P("dp"),
        P("dp"),
        P("dp"),
        P("dp", None),
        P(None, "dp", "tensor"),
        P(None, "tensor"),
        P(None, "tensor", "dp"),
        P(None, "dp"),
        P("dp", None, None),
        P("dp", None, None),
        P(("dp", "tensor"), None, None),
    )
    return jax.shard_map(
        per_device,
        mesh=mesh,
        in_specs=placed,
        out_specs=(
            P(("dp", "tensor"), None, None),
            P(("dp", "tensor"), None, None),
            P("dp"),
            P("dp"),
            P("dp", None, "tensor"),
            P("tensor", "dp"),
            P("dp"),
            P("dp"),
            P("dp"),
            P("dp", None),
            P(None, "dp", "tensor"),
            P(None, ("dp", "tensor")),
            P(None, "tensor", "dp"),
            P(None, "dp"),
        ),
        check_vma=False,
    )
```

```python
import functools

import jax
import jax.numpy as jnp
from jax import lax
from jax.experimental import pallas as pl
from jax.experimental.pallas import tpu as pltpu
from jax.sharding import PartitionSpec as P

HEAD_DIM = 64
SEQ = 197


EPSILON = 1e-06
PRECISE = lax.Precision.HIGHEST


MESH = pl.DeviceIdType.MESH
LINE = 4
SIDE = 2


def greet(z, y, tensor):
    barrier = pltpu.get_barrier_semaphore()
    pl.semaphore_signal(
        barrier, inc=1, device_id=(z * SIDE + 1 - y, tensor), device_id_type=MESH
    )

    @pl.when(z > 0)
    def _():
        pl.semaphore_signal(
            barrier, inc=1, device_id=((z - 1) * SIDE + y, tensor), device_id_type=MESH
        )

    @pl.when(z < LINE - 1)
    def _():
        pl.semaphore_signal(
            barrier, inc=1, device_id=((z + 1) * SIDE + y, tensor), device_id_type=MESH
        )

    @pl.when((z == 0) | (z == LINE - 1))
    def _():
        pl.semaphore_wait(barrier, 2)

    @pl.when((z > 0) & (z < LINE - 1))
    def _():
        pl.semaphore_wait(barrier, 3)


def gather_kernel(count, *refs):
    sources = refs[:count]
    outs = refs[count : 2 * count]
    own_sem, side_send, up_send, down_send, arrived = refs[2 * count :]
    place = lax.axis_index("dp")
    tensor = lax.axis_index("tensor")
    z = place // SIDE
    y = place % SIDE
    greet(z, y, tensor)

    def send(piece, block, level, column, send_sem, first):
        where = outs[piece].at[:, block]
        return pltpu.make_async_remote_copy(
            src_ref=sources[piece] if first else where,
            dst_ref=where,
            send_sem=send_sem,
            recv_sem=arrived.at[piece, block],
            device_id=(level * SIDE + column, tensor),
            device_id_type=MESH,
        )

    def to_side(piece, level, first=False):
        return send(
            piece, level * SIDE + y, z, 1 - y, side_send.at[piece, level], first
        )

    def to_up(piece, level, first=False):
        return send(piece, level * SIDE + y, z + 1, y, up_send.at[piece, level], first)

    def to_down(piece, level, first=False):
        return send(piece, level * SIDE + y, z - 1, y, down_send.at[piece, level], first)

    for piece in range(count):

        @pl.when(z < LINE - 1)
        def _():
            to_up(piece, z, True).start()

        @pl.when(z > 0)
        def _():
            to_down(piece, z, True).start()

        to_side(piece, z, True).start()
        pltpu.make_async_copy(
            sources[piece], outs[piece].at[:, place], own_sem.at[piece]
        ).start()
    for step in range(1, LINE):
        for piece in range(count):

            @pl.when(z - step >= 0)
            def _():
                came = to_down(piece, z - step)
                came.wait_recv()

                @pl.when(z < LINE - 1)
                def _():
                    to_up(piece, z - step).start()

                to_side(piece, z - step).start()

            @pl.when(z + step <= LINE - 1)
            def _():
                came = to_up(piece, z + step)
                came.wait_recv()

                @pl.when(z > 0)
                def _():
                    to_down(piece, z + step).start()

                to_side(piece, z + step).start()

    for piece in range(count):
        pltpu.make_async_copy(
            sources[piece], outs[piece].at[:, place], own_sem.at[piece]
        ).wait()
        for level in range(LINE):
            send(
                piece, level * SIDE + 1 - y, z, 1 - y, side_send.at[piece, level], False
            ).wait_recv()
            to_side(piece, level).wait_send()

            @pl.when((z < LINE - 1) & (level <= z))
            def _():
                to_up(piece, level).wait_send()

            @pl.when((z > 0) & (level >= z))
            def _():
                to_down(piece, level).wait_send()


def gather_weights(*shards):
    count = len(shards)
    return pl.pallas_call(
        functools.partial(gather_kernel, count),
        out_shape=[
            jax.ShapeDtypeStruct(
                (shard.shape[0], LINE * SIDE) + shard.shape[1:], shard.dtype
            )
            for shard in shards
        ],
        in_specs=[pl.BlockSpec(memory_space=pl.ANY)] * count,
        out_specs=[pl.BlockSpec(memory_space=pl.ANY)] * count,
        scratch_shapes=[
            pltpu.SemaphoreType.DMA((count,)),
            pltpu.SemaphoreType.DMA((count, LINE)),
            pltpu.SemaphoreType.DMA((count, LINE)),
            pltpu.SemaphoreType.DMA((count, LINE)),
            pltpu.SemaphoreType.DMA((count, LINE * SIDE)),
        ],
        compiler_params=pltpu.CompilerParams(collective_id=0, has_side_effects=True),
    )(*shards)


def reduce_kernel(count, *refs):
    terms = refs[:count]
    outs = refs[count : 2 * count]
    side_in = refs[2 * count : 3 * count]
    line_in = refs[3 * count : 4 * count]
    passing = refs[4 * count : 5 * count]
    side_send, side_recv, line_send, line_recv = refs[5 * count :]
    place = lax.axis_index("dp")
    tensor = lax.axis_index("tensor")
    z = place // SIDE
    y = place % SIDE
    greet(z, y, tensor)
    high = z // 2
    depth = z + high * (3 - 2 * z)
    inward = 1 - 2 * high
    end = depth == 0
    middle = depth == 1

    def target(step):
        mirrored = (3, 2, 1 - depth, depth)[step]
        return mirrored + high * (3 - 2 * mirrored)

    def to_side(piece, step):
        return pltpu.make_async_remote_copy(
            src_ref=terms[piece].at[:, target(step) * SIDE + 1 - y],
            dst_ref=side_in[piece].at[step],
            send_sem=side_send.at[piece, step],
            recv_sem=side_recv.at[piece, step],
            device_id=(z * SIDE + 1 - y, tensor),
            device_id_type=MESH,
        )

    def to_line(piece, step, slot, move):
        return pltpu.make_async_remote_copy(
            src_ref=passing[piece].at[step],
            dst_ref=line_in[piece].at[slot],
            send_sem=line_send.at[piece, step],
            recv_sem=line_recv.at[piece, slot],
            device_id=((z + move) * SIDE + y, tensor),
            device_id_type=MESH,
        )

    def add(piece, step, slots, dst):
        slabs, _, rows, _ = terms[piece].shape
        mine = terms[piece].at[:, target(step) * SIDE + y]
        per = rows // 16

        @pl.loop(0, slabs * per)
        def _(at):
            slab = at // per
            part = pl.ds(pl.multiple_of((at % per) * 16, 16), 16)
            total = mine[slab, part, :].astype(jnp.float32)
            total += side_in[piece][step, slab, part, :].astype(jnp.float32)
            for slot in slots:
                total += line_in[piece][slot, slab, part, :].astype(jnp.float32)
            dst[slab, part, :] = total.astype(dst.dtype)

    for step in range(4):
        for piece in range(count):
            to_side(piece, step).start()

    for step in range(4):
        for piece in range(count):
            to_side(piece, step).wait_recv()
            if step < 3:

                @pl.when(end)
                def _():
                    add(piece, step, (), passing[piece].at[step])
                    to_line(piece, step, step, inward).start()

                @pl.when(middle)
                def _():
                    slot = (0, 1, 3)[step]
                    to_line(piece, step, slot, inward).wait_recv()
                    add(piece, step, (slot,), passing[piece].at[step])
                    if step < 2:
                        to_line(piece, step, 3 + step, inward).start()
                    else:
                        to_line(piece, step, 4, -inward).start()

            else:

                @pl.when(end)
                def _():
                    to_line(piece, 0, 4, inward).wait_recv()
                    add(piece, step, (4,), outs[piece])

                @pl.when(middle)
                def _():
                    to_line(piece, 0, 2, inward).wait_recv()
                    to_line(piece, 0, 4, inward).wait_recv()
                    add(piece, step, (2, 4), outs[piece])

    for piece in range(count):
        for step in range(4):
            to_side(piece, step).wait_send()
        for step in range(3):
            to_line(piece, step, step, inward).wait_send()


def reduce_grads(*terms):
    count = len(terms)
    shards = [(term.shape[0],) + term.shape[2:] for term in terms]
    return pl.pallas_call(
        functools.partial(reduce_kernel, count),
        out_shape=[jax.ShapeDtypeStruct(shard, jnp.float32) for shard in shards],
        in_specs=[pl.BlockSpec(memory_space=pltpu.VMEM)] * count,
        out_specs=[pl.BlockSpec(memory_space=pltpu.VMEM)] * count,
        scratch_shapes=[pltpu.VMEM((4,) + shard, jnp.bfloat16) for shard in shards]
        + [pltpu.VMEM((5,) + shard, jnp.bfloat16) for shard in shards]
        + [pltpu.VMEM((3,) + shard, jnp.bfloat16) for shard in shards]
        + [
            pltpu.SemaphoreType.DMA((count, 4)),
            pltpu.SemaphoreType.DMA((count, 4)),
            pltpu.SemaphoreType.DMA((count, 3)),
            pltpu.SemaphoreType.DMA((count, 5)),
        ],
        compiler_params=pltpu.CompilerParams(
            collective_id=1, has_side_effects=True, vmem_limit_bytes=52 * 2**20
        ),
    )(*terms)


def layer_norm(values, gain, bias):
    centred = values - jnp.mean(values, axis=-1, keepdims=True)
    spread = jnp.mean(centred * centred, axis=-1, keepdims=True)
    return centred * lax.rsqrt(spread + EPSILON) * gain + bias


def gelu_tanh(values):
    return jax.nn.gelu(values, approximate=True)


def per_device(
    inputs,
    ln1_gain,
    ln1_bias,
    qkv_weight,
    proj_weight,
    proj_bias,
    ln2_gain,
    ln2_bias,
    router_weight,
    expert_in,
    expert_in_bias,
    expert_out,
    expert_out_bias,
    expert_ids,
    slot_ids,
    cotangent,
):
    local_images, seq_len, model_width = inputs.shape
    tensor_count = lax.axis_size("tensor")
    dp_count = lax.axis_size("dp")
    tensor_rank = lax.axis_index("tensor")
    dp_rank = lax.axis_index("dp")
    group_images = local_images * tensor_count
    experts = expert_in.shape[0]
    tokens = group_images * SEQ
    slot_count = 40 * tokens // (19 * experts) + 1
    slot_rows = -(-slot_count // 16) * 16
    heads_local = qkv_weight.shape[2] // HEAD_DIM
    score_scale = HEAD_DIM ** (-0.5)

    def own_rows(values):
        return lax.dynamic_slice_in_dim(values, tensor_rank * local_images, local_images, 0)

    def scatter_rows(values):
        return lax.psum_scatter(
            values.astype(jnp.bfloat16), "tensor", scatter_dimension=0, tiled=True
        ).astype(jnp.float32)

    def split_three(values):
        first = values.astype(jnp.bfloat16)
        rest = values - first.astype(jnp.float32)
        second = rest.astype(jnp.bfloat16)
        third = (rest - second.astype(jnp.float32)).astype(jnp.bfloat16)
        return jnp.concatenate([first, second, third], axis=-1)

    share = model_width // dp_count
    by_kernel = dp_count == LINE * SIDE and tensor_count == 4

    def over_dp(shard):
        return lax.all_gather(shard, "dp", axis=1)

    attn_shard = jnp.concatenate(
        [qkv_weight.reshape(share, -1), proj_weight.T], axis=1
    )[None]
    small_shard = jnp.concatenate(
        [
            jnp.stack([ln1_gain, ln1_bias, proj_bias, ln2_gain, ln2_bias], axis=1),
            router_weight,
            expert_out_bias.T,
        ],
        axis=1,
    )
    small_shard = jnp.pad(small_shard, ((0, 0), (0, 128 - small_shard.shape[1])))[None]
    shards = (
        small_shard,
        attn_shard,
        expert_in,
        jnp.swapaxes(expert_out, 1, 2),
    )
    if by_kernel:
        fetched = gather_weights(*shards)
    else:
        fetched = [over_dp(shard) for shard in shards]
    small_full = fetched[0].reshape(model_width, 128)
    attn_full = fetched[1].reshape(model_width, -1)
    in_full = fetched[2].reshape(experts, model_width, -1)
    out_full = fetched[3].reshape(experts, model_width, -1)
    qkv_cols = 3 * heads_local * HEAD_DIM
    qkv_full = attn_full[:, :qkv_cols].reshape(model_width, 3, -1)
    proj_full = attn_full[:, qkv_cols:]
    gain_one, bias_one, proj_shift, gain_two, bias_two = (small_full[:, k] for k in range(5))
    router_full = small_full[:, 5 : 5 + experts]
    back_shift = small_full[:, 5 + experts : 5 + 2 * experts].T

    def scores_of(query_heads, key_heads):
        return (
            jnp.einsum(
                "bqhe,bkhe->bhqk", query_heads, key_heads, preferred_element_type=jnp.float32
            )
            * score_scale
        )

    gain_one_f = gain_one.astype(jnp.float32)
    bias_one_f = bias_one.astype(jnp.float32)
    source = inputs.astype(jnp.float32)
    normed_one = layer_norm(source, gain_one_f, bias_one_f).astype(jnp.bfloat16)
    rows_one = lax.all_gather(normed_one, "tensor", axis=0, tiled=True)
    mixed = jnp.einsum(
        "bsd,dkf->bskf", rows_one, qkv_full, preferred_element_type=jnp.float32
    ).astype(jnp.bfloat16)
    head_blocks = mixed.reshape(group_images, seq_len, 3, heads_local, HEAD_DIM)
    query_heads = head_blocks[:, :, 0]
    key_heads = head_blocks[:, :, 1]
    value_heads = head_blocks[:, :, 2]
    scores = scores_of(query_heads, key_heads)
    top_score = jnp.max(scores, axis=-1, keepdims=True)
    raised = jnp.exp(scores - top_score)
    row_total = jnp.sum(raised, axis=-1, keepdims=True)
    weights = raised / row_total
    log_total = top_score + jnp.log(row_total)
    attended = jnp.einsum(
        "bhqk,bkhe->bqhe",
        weights.astype(jnp.bfloat16),
        value_heads,
        preferred_element_type=jnp.float32,
    )
    attended = attended.astype(jnp.bfloat16).reshape(group_images, seq_len, heads_local * HEAD_DIM)
    attn_terms = jnp.einsum("bsf,df->bsd", attended, proj_full, preferred_element_type=jnp.float32)
    attn_sum = scatter_rows(attn_terms)
    state = source + attn_sum + proj_shift.astype(jnp.float32)
    gain_two_f = gain_two.astype(jnp.float32)
    bias_two_f = bias_two.astype(jnp.float32)
    normed_two = layer_norm(state, gain_two_f, bias_two_f).astype(jnp.bfloat16)
    rows_two = lax.all_gather(normed_two, "tensor", axis=0, tiled=True)
    out_rows = lax.all_gather(cotangent, "tensor", axis=0, tiled=True)
    token_rows = rows_two.reshape(tokens, model_width)
    grad_rows = out_rows.reshape(tokens, model_width)
    choice_ids = expert_ids.reshape(tokens, 2)
    places = choice_ids * slot_rows + slot_ids.reshape(tokens, 2)
    slot_index = jnp.arange(experts * slot_rows, dtype=jnp.int32)[:, None]
    chosen = (
        (slot_index == places[:, 0][None, :]) | (slot_index == places[:, 1][None, :])
    ).astype(jnp.bfloat16)
    logits = jnp.dot(token_rows, router_full, preferred_element_type=jnp.float32)
    router_probs = jax.nn.softmax(logits, axis=-1)
    expert_mask = (
        jnp.arange(experts * slot_rows)[:, None] // slot_rows == jnp.arange(experts)[None, :]
    )
    slot_probs = jnp.dot(chosen, split_three(router_probs), preferred_element_type=jnp.float32)
    slot_gates = jnp.sum(
        jnp.where(expert_mask[:, None, :], slot_probs.reshape(-1, 3, experts), 0.0), axis=(1, 2)
    )
    dispatched = (
        jnp.dot(chosen, token_rows, preferred_element_type=jnp.float32)
        .astype(jnp.bfloat16)
        .reshape(experts, slot_rows, model_width)
    )
    slot_out = (
        jnp.dot(chosen, grad_rows, preferred_element_type=jnp.float32)
    )
    slot_grad = (
        (slot_gates[:, None] * slot_out)
        .astype(jnp.bfloat16)
        .reshape(experts, slot_rows, model_width)
    )
    pre = (
        jnp.einsum("ecd,edf->ecf", dispatched, in_full, preferred_element_type=jnp.float32)
        + expert_in_bias.astype(jnp.float32)[:, None, :]
    )
    hidden = gelu_tanh(pre).astype(jnp.bfloat16)
    expert_terms = jnp.einsum(
        "ecf,edf->ecd", hidden, out_full, preferred_element_type=jnp.float32
    ).reshape(experts * slot_rows, model_width)
    gated_terms = (slot_gates[:, None] * expert_terms).astype(jnp.bfloat16)
    slot_dgate = jnp.sum(expert_terms * slot_out, axis=-1)
    mixed_terms = jnp.einsum(
        "st,sd->td", chosen, gated_terms, preferred_element_type=jnp.float32
    )
    mixed_sum = scatter_rows(mixed_terms.reshape(group_images, seq_len, model_width))
    own_ids = own_rows(expert_ids.reshape(group_images, seq_len, 2))
    onehot_own = (own_ids[..., None] == jnp.arange(experts)).astype(jnp.float32)
    probs_own = own_rows(router_probs.reshape(group_images, seq_len, experts))
    probs_chosen = probs_own * jnp.sum(onehot_own, axis=2)
    back_f = back_shift.astype(jnp.float32)
    shift_own = jnp.einsum("bpe,ed->bpd", probs_chosen, back_f, precision=PRECISE)
    result = state + mixed_sum + shift_own
    block_out = result.astype(jnp.bfloat16)
    own_grad = cotangent.astype(jnp.float32)
    out_grad = jnp.einsum("ecf,ecd->edf", hidden, slot_grad, preferred_element_type=jnp.float32)
    hidden_grad = jnp.einsum(
        "ecd,edf->ecf", slot_grad, out_full, preferred_element_type=jnp.float32
    )
    gelu_pull = jax.vjp(gelu_tanh, pre)[1]
    pre_grad = gelu_pull(hidden_grad)[0].astype(jnp.bfloat16)
    in_grad = jnp.einsum("ecd,ecf->edf", dispatched, pre_grad, preferred_element_type=jnp.float32)
    in_bias_grad = jnp.sum(pre_grad.astype(jnp.float32), axis=1)
    slot_back = (
        jnp.einsum("ecf,edf->ecd", pre_grad, in_full, preferred_element_type=jnp.float32)
        .astype(jnp.bfloat16)
        .reshape(experts * slot_rows, model_width)
    )
    row_back = jnp.einsum("st,sd->td", chosen, slot_back, preferred_element_type=jnp.float32)
    dgate_cols = split_three(jnp.where(expert_mask, slot_dgate[:, None], 0.0))
    prob_parts = jnp.sum(
        jnp.einsum("st,sk->tk", chosen, dgate_cols, preferred_element_type=jnp.float32).reshape(
            tokens, 3, experts
        ),
        axis=1,
    )
    row_sum = scatter_rows(row_back.reshape(group_images, seq_len, model_width))
    prob_sum = lax.psum_scatter(
        prob_parts.reshape(group_images, seq_len, experts),
        "tensor",
        scatter_dimension=0,
        tiled=True,
    )
    prob_grad = prob_sum + jnp.sum(onehot_own, axis=2) * jnp.einsum(
        "bpd,ed->bpe", own_grad, back_f, precision=PRECISE
    )
    logit_grad = probs_own * (prob_grad - jnp.sum(probs_own * prob_grad, axis=-1, keepdims=True))
    normed_grad = row_sum + jnp.einsum(
        "bpe,de->bpd", logit_grad, router_full.astype(jnp.float32), precision=PRECISE
    )
    router_grad = jnp.einsum(
        "bpd,bpe->de", normed_two.astype(jnp.float32), logit_grad, precision=PRECISE
    )
    back_bias_grad = jnp.einsum("bpe,bpd->ed", probs_chosen, own_grad, precision=PRECISE)
    norm_two_pull = jax.vjp(layer_norm, state, gain_two_f, bias_two_f)[1]
    state_grad, gain_two_grad, bias_two_grad = norm_two_pull(normed_grad)
    state_grad = state_grad + own_grad
    proj_bias_grad = jnp.sum(state_grad, axis=(0, 1))
    state_rows = lax.all_gather(state_grad.astype(jnp.bfloat16), "tensor", axis=0, tiled=True)
    proj_grad = jnp.einsum("bsf,bsd->df", attended, state_rows, preferred_element_type=jnp.float32)
    attended_grad = jnp.einsum(
        "bsd,df->bsf", state_rows, proj_full, preferred_element_type=jnp.float32
    )
    attended_grad = attended_grad.astype(jnp.bfloat16).reshape(
        group_images, seq_len, heads_local, HEAD_DIM
    )
    weight_grad = jnp.einsum(
        "bqhe,bkhe->bhqk", attended_grad, value_heads, preferred_element_type=jnp.float32
    )
    centre = jnp.sum(weights * weight_grad, axis=-1, keepdims=True)
    score_grad = (weights * (weight_grad - centre)).astype(jnp.bfloat16)
    query_grad = (
        jnp.einsum("bhqk,bkhe->bqhe", score_grad, key_heads, preferred_element_type=jnp.float32)
        * score_scale
    )
    key_grad = (
        jnp.einsum("bhqk,bqhe->bkhe", score_grad, query_heads, preferred_element_type=jnp.float32)
        * score_scale
    )
    value_grad = jnp.einsum(
        "bhqk,bqhe->bkhe",
        weights.astype(jnp.bfloat16),
        attended_grad,
        preferred_element_type=jnp.float32,
    )
    heads_grad = jnp.stack([query_grad, key_grad, value_grad], axis=2).astype(jnp.bfloat16)
    heads_grad = heads_grad.reshape(group_images, seq_len, 3, heads_local * HEAD_DIM)
    qkv_grad = jnp.einsum("bsd,bskf->dkf", rows_one, heads_grad, preferred_element_type=jnp.float32)
    rows_grad = jnp.einsum(
        "bskf,dkf->bsd", heads_grad, qkv_full, preferred_element_type=jnp.float32
    )
    normed_one_grad = scatter_rows(rows_grad)
    norm_one_pull = jax.vjp(layer_norm, source, gain_one_f, bias_one_f)[1]
    source_grad, gain_one_grad, bias_one_grad = norm_one_pull(normed_one_grad)
    input_grad = state_grad + source_grad
    hidden_cols = in_bias_grad.shape[1]
    bias_share = hidden_cols // dp_count
    attn_grad = jnp.concatenate(
        [qkv_grad.reshape(model_width, qkv_cols), proj_grad], axis=1
    )
    small_grad = jnp.concatenate(
        [
            jnp.stack(
                [gain_one_grad, bias_one_grad, proj_bias_grad, gain_two_grad, bias_two_grad],
                axis=1,
            ),
            router_grad,
            back_bias_grad.T,
            in_bias_grad.T,
        ],
        axis=1,
    )
    small_grad = jnp.pad(small_grad, ((0, 0), (0, 128 - small_grad.shape[1])))

    def blocks(values):
        return values.astype(jnp.bfloat16).reshape(
            -1, dp_count, values.shape[-2] // dp_count, values.shape[-1]
        )

    grads = [blocks(values) for values in (small_grad, attn_grad, in_grad, out_grad)]
    if by_kernel:
        small_part, attn_part, in_part, out_part = reduce_grads(*grads)
    else:
        small_part, attn_part, in_part, out_part = (
            lax.psum_scatter(values, "dp", scatter_dimension=1).astype(jnp.float32)
            for values in grads
        )
    small_part = small_part[0]
    norm_cols = 5 + 2 * experts
    totals = lax.psum(small_part[:, :norm_cols], "tensor")
    moves = []
    for source_dp in range(dp_count):
        for source_tensor in range(tensor_count):
            moves.append(
                (source_dp * tensor_count + source_tensor, source_tensor * dp_count + source_dp)
            )
    in_bias_out = lax.ppermute(
        small_part[:, norm_cols : norm_cols + experts].T, ("dp", "tensor"), moves
    )
    attn_part = attn_part[0]
    return (
        block_out,
        input_grad,
        totals[:, 0],
        totals[:, 1],
        attn_part[:, :qkv_cols].reshape(share, 3, -1),
        attn_part[:, qkv_cols:].T,
        totals[:, 2],
        totals[:, 3],
        totals[:, 4],
        totals[:, 5 : 5 + experts],
        in_part,
        in_bias_out,
        jnp.swapaxes(out_part, 1, 2),
        totals[:, 5 + experts : norm_cols].T,
    )


def solution(mesh):
    placed = (
        P(("dp", "tensor"), None, None),
        P("dp"),
        P("dp"),
        P("dp", None, "tensor"),
        P("tensor", "dp"),
        P("dp"),
        P("dp"),
        P("dp"),
        P("dp", None),
        P(None, "dp", "tensor"),
        P(None, "tensor"),
        P(None, "tensor", "dp"),
        P(None, "dp"),
        P("dp", None, None),
        P("dp", None, None),
        P(("dp", "tensor"), None, None),
    )
    return jax.shard_map(
        per_device,
        mesh=mesh,
        in_specs=placed,
        out_specs=(
            P(("dp", "tensor"), None, None),
            P(("dp", "tensor"), None, None),
            P("dp"),
            P("dp"),
            P("dp", None, "tensor"),
            P("tensor", "dp"),
            P("dp"),
            P("dp"),
            P("dp"),
            P("dp", None),
            P(None, "dp", "tensor"),
            P(None, ("dp", "tensor")),
            P(None, "tensor", "dp"),
            P(None, "dp"),
        ),
        check_vma=False,
    )
```

```python
import functools

import jax
import jax.numpy as jnp
from jax import lax
from jax.experimental import pallas as pl
from jax.experimental.pallas import tpu as pltpu
from jax.sharding import PartitionSpec as P

HEAD_DIM = 64
SEQ = 197


EPSILON = 1e-06
PRECISE = lax.Precision.HIGHEST


MESH = pl.DeviceIdType.MESH
LINE = 4
SIDE = 2


def greet(z, y, tensor):
    barrier = pltpu.get_barrier_semaphore()
    pl.semaphore_signal(
        barrier, inc=1, device_id=(z * SIDE + 1 - y, tensor), device_id_type=MESH
    )

    @pl.when(z > 0)
    def _():
        pl.semaphore_signal(
            barrier, inc=1, device_id=((z - 1) * SIDE + y, tensor), device_id_type=MESH
        )

    @pl.when(z < LINE - 1)
    def _():
        pl.semaphore_signal(
            barrier, inc=1, device_id=((z + 1) * SIDE + y, tensor), device_id_type=MESH
        )

    @pl.when((z == 0) | (z == LINE - 1))
    def _():
        pl.semaphore_wait(barrier, 2)

    @pl.when((z > 0) & (z < LINE - 1))
    def _():
        pl.semaphore_wait(barrier, 3)


def gather_kernel(count, *refs):
    sources = refs[:count]
    outs = refs[count : 2 * count]
    own_sem, side_send, up_send, down_send, arrived = refs[2 * count :]
    place = lax.axis_index("dp")
    tensor = lax.axis_index("tensor")
    z = place // SIDE
    y = place % SIDE
    greet(z, y, tensor)

    def send(piece, block, level, column, send_sem, first):
        where = outs[piece].at[:, block]
        return pltpu.make_async_remote_copy(
            src_ref=sources[piece] if first else where,
            dst_ref=where,
            send_sem=send_sem,
            recv_sem=arrived.at[piece, block],
            device_id=(level * SIDE + column, tensor),
            device_id_type=MESH,
        )

    def to_side(piece, level, first=False):
        return send(
            piece, level * SIDE + y, z, 1 - y, side_send.at[piece, level], first
        )

    def to_up(piece, level, first=False):
        return send(piece, level * SIDE + y, z + 1, y, up_send.at[piece, level], first)

    def to_down(piece, level, first=False):
        return send(piece, level * SIDE + y, z - 1, y, down_send.at[piece, level], first)

    for piece in range(count):

        @pl.when(z < LINE - 1)
        def _():
            to_up(piece, z, True).start()

        @pl.when(z > 0)
        def _():
            to_down(piece, z, True).start()

        to_side(piece, z, True).start()
        pltpu.make_async_copy(
            sources[piece], outs[piece].at[:, place], own_sem.at[piece]
        ).start()
    for step in range(1, LINE):
        for piece in range(count):

            @pl.when(z - step >= 0)
            def _():
                came = to_down(piece, z - step)
                came.wait_recv()

                @pl.when(z < LINE - 1)
                def _():
                    to_up(piece, z - step).start()

                to_side(piece, z - step).start()

            @pl.when(z + step <= LINE - 1)
            def _():
                came = to_up(piece, z + step)
                came.wait_recv()

                @pl.when(z > 0)
                def _():
                    to_down(piece, z + step).start()

                to_side(piece, z + step).start()

    for piece in range(count):
        pltpu.make_async_copy(
            sources[piece], outs[piece].at[:, place], own_sem.at[piece]
        ).wait()
        for level in range(LINE):
            send(
                piece, level * SIDE + 1 - y, z, 1 - y, side_send.at[piece, level], False
            ).wait_recv()
            to_side(piece, level).wait_send()

            @pl.when((z < LINE - 1) & (level <= z))
            def _():
                to_up(piece, level).wait_send()

            @pl.when((z > 0) & (level >= z))
            def _():
                to_down(piece, level).wait_send()


def gather_weights(*shards):
    count = len(shards)
    return pl.pallas_call(
        functools.partial(gather_kernel, count),
        out_shape=[
            jax.ShapeDtypeStruct(
                (shard.shape[0], LINE * SIDE) + shard.shape[1:], shard.dtype
            )
            for shard in shards
        ],
        in_specs=[pl.BlockSpec(memory_space=pl.ANY)] * count,
        out_specs=[pl.BlockSpec(memory_space=pl.ANY)] * count,
        scratch_shapes=[
            pltpu.SemaphoreType.DMA((count,)),
            pltpu.SemaphoreType.DMA((count, LINE)),
            pltpu.SemaphoreType.DMA((count, LINE)),
            pltpu.SemaphoreType.DMA((count, LINE)),
            pltpu.SemaphoreType.DMA((count, LINE * SIDE)),
        ],
        compiler_params=pltpu.CompilerParams(collective_id=0, has_side_effects=True),
        cost_estimate=pl.CostEstimate(
            flops=0, bytes_accessed=400_000_000, transcendentals=0
        ),
    )(*shards)


def reduce_kernel(count, *refs):
    terms = refs[:count]
    outs = refs[count : 2 * count]
    side_in = refs[2 * count : 3 * count]
    line_in = refs[3 * count : 4 * count]
    passing = refs[4 * count : 5 * count]
    side_send, side_recv, line_send, line_recv = refs[5 * count :]
    place = lax.axis_index("dp")
    tensor = lax.axis_index("tensor")
    z = place // SIDE
    y = place % SIDE
    greet(z, y, tensor)
    high = z // 2
    depth = z + high * (3 - 2 * z)
    inward = 1 - 2 * high
    end = depth == 0
    middle = depth == 1

    def target(step):
        mirrored = (3, 2, 1 - depth, depth)[step]
        return mirrored + high * (3 - 2 * mirrored)

    def to_side(piece, step):
        return pltpu.make_async_remote_copy(
            src_ref=terms[piece].at[:, target(step) * SIDE + 1 - y],
            dst_ref=side_in[piece].at[step],
            send_sem=side_send.at[piece, step],
            recv_sem=side_recv.at[piece, step],
            device_id=(z * SIDE + 1 - y, tensor),
            device_id_type=MESH,
        )

    def to_line(piece, step, slot, move):
        return pltpu.make_async_remote_copy(
            src_ref=passing[piece].at[step],
            dst_ref=line_in[piece].at[slot],
            send_sem=line_send.at[piece, step],
            recv_sem=line_recv.at[piece, slot],
            device_id=((z + move) * SIDE + y, tensor),
            device_id_type=MESH,
        )

    def add(piece, step, slots, dst):
        slabs, _, rows, _ = terms[piece].shape
        mine = terms[piece].at[:, target(step) * SIDE + y]
        per = rows // 16

        @pl.loop(0, slabs * per)
        def _(at):
            slab = at // per
            part = pl.ds(pl.multiple_of((at % per) * 16, 16), 16)
            total = mine[slab, part, :].astype(jnp.float32)
            total += side_in[piece][step, slab, part, :].astype(jnp.float32)
            for slot in slots:
                total += line_in[piece][slot, slab, part, :].astype(jnp.float32)
            dst[slab, part, :] = total.astype(dst.dtype)

    for step in range(4):
        for piece in range(count):
            to_side(piece, step).start()

    for step in range(4):
        for piece in range(count):
            to_side(piece, step).wait_recv()
            if step < 3:

                @pl.when(end)
                def _():
                    add(piece, step, (), passing[piece].at[step])
                    to_line(piece, step, step, inward).start()

                @pl.when(middle)
                def _():
                    slot = (0, 1, 3)[step]
                    to_line(piece, step, slot, inward).wait_recv()
                    add(piece, step, (slot,), passing[piece].at[step])
                    if step < 2:
                        to_line(piece, step, 3 + step, inward).start()
                    else:
                        to_line(piece, step, 4, -inward).start()

            else:

                @pl.when(end)
                def _():
                    to_line(piece, 0, 4, inward).wait_recv()
                    add(piece, step, (4,), outs[piece])

                @pl.when(middle)
                def _():
                    to_line(piece, 0, 2, inward).wait_recv()
                    to_line(piece, 0, 4, inward).wait_recv()
                    add(piece, step, (2, 4), outs[piece])

    for piece in range(count):
        for step in range(4):
            to_side(piece, step).wait_send()
        for step in range(3):
            to_line(piece, step, step, inward).wait_send()


def reduce_grads(*terms):
    count = len(terms)
    shards = [(term.shape[0],) + term.shape[2:] for term in terms]
    return pl.pallas_call(
        functools.partial(reduce_kernel, count),
        out_shape=[jax.ShapeDtypeStruct(shard, jnp.float32) for shard in shards],
        in_specs=[pl.BlockSpec(memory_space=pltpu.VMEM)] * count,
        out_specs=[pl.BlockSpec(memory_space=pltpu.VMEM)] * count,
        scratch_shapes=[pltpu.VMEM((4,) + shard, jnp.bfloat16) for shard in shards]
        + [pltpu.VMEM((5,) + shard, jnp.bfloat16) for shard in shards]
        + [pltpu.VMEM((3,) + shard, jnp.bfloat16) for shard in shards]
        + [
            pltpu.SemaphoreType.DMA((count, 4)),
            pltpu.SemaphoreType.DMA((count, 4)),
            pltpu.SemaphoreType.DMA((count, 3)),
            pltpu.SemaphoreType.DMA((count, 5)),
        ],
        compiler_params=pltpu.CompilerParams(
            collective_id=1, has_side_effects=True, vmem_limit_bytes=52 * 2**20
        ),
    )(*terms)


def layer_norm(values, gain, bias):
    centred = values - jnp.mean(values, axis=-1, keepdims=True)
    spread = jnp.mean(centred * centred, axis=-1, keepdims=True)
    return centred * lax.rsqrt(spread + EPSILON) * gain + bias


def gelu_tanh(values):
    return jax.nn.gelu(values, approximate=True)


def per_device(
    inputs,
    ln1_gain,
    ln1_bias,
    qkv_weight,
    proj_weight,
    proj_bias,
    ln2_gain,
    ln2_bias,
    router_weight,
    expert_in,
    expert_in_bias,
    expert_out,
    expert_out_bias,
    expert_ids,
    slot_ids,
    cotangent,
):
    local_images, seq_len, model_width = inputs.shape
    tensor_count = lax.axis_size("tensor")
    dp_count = lax.axis_size("dp")
    tensor_rank = lax.axis_index("tensor")
    dp_rank = lax.axis_index("dp")
    group_images = local_images * tensor_count
    experts = expert_in.shape[0]
    tokens = group_images * SEQ
    slot_count = 40 * tokens // (19 * experts) + 1
    slot_rows = -(-slot_count // 16) * 16
    heads_local = qkv_weight.shape[2] // HEAD_DIM
    score_scale = HEAD_DIM ** (-0.5)

    def own_rows(values):
        return lax.dynamic_slice_in_dim(values, tensor_rank * local_images, local_images, 0)

    def scatter_rows(values):
        low = values.astype(jnp.bfloat16)
        total = own_rows(values)
        for hop in range(1, tensor_count):
            there = lax.rem(tensor_rank + hop, tensor_count)
            part = lax.dynamic_slice_in_dim(low, there * local_images, local_images, 0)
            ring = [(rank, (rank + hop) % tensor_count) for rank in range(tensor_count)]
            total = total + lax.ppermute(part, "tensor", ring).astype(jnp.float32)
        return total

    def split_three(values):
        first = values.astype(jnp.bfloat16)
        rest = values - first.astype(jnp.float32)
        second = rest.astype(jnp.bfloat16)
        third = (rest - second.astype(jnp.float32)).astype(jnp.bfloat16)
        return jnp.concatenate([first, second, third], axis=-1)

    share = model_width // dp_count
    both_rows = lax.all_gather(
        jnp.stack([inputs, cotangent], axis=1), "tensor", axis=0, tiled=True
    )
    by_kernel = dp_count == LINE * SIDE and tensor_count == 4

    def over_dp(shard):
        return lax.all_gather(shard, "dp", axis=1)

    attn_shard = jnp.concatenate(
        [qkv_weight.reshape(share, -1), proj_weight.T], axis=1
    )[None]
    small_shard = jnp.concatenate(
        [
            jnp.stack([ln1_gain, ln1_bias, proj_bias, ln2_gain, ln2_bias], axis=1),
            router_weight,
            expert_out_bias.T,
        ],
        axis=1,
    )
    small_shard = jnp.pad(small_shard, ((0, 0), (0, 128 - small_shard.shape[1])))[None]
    shards = (
        small_shard,
        attn_shard,
        expert_in,
        jnp.swapaxes(expert_out, 1, 2),
    )
    if by_kernel:
        fetched = gather_weights(*shards)
    else:
        fetched = [over_dp(shard) for shard in shards]
    small_full = fetched[0].reshape(model_width, 128)
    attn_full = fetched[1].reshape(model_width, -1)
    in_full = fetched[2].reshape(experts, model_width, -1)
    out_full = fetched[3].reshape(experts, model_width, -1)
    qkv_cols = 3 * heads_local * HEAD_DIM
    qkv_full = attn_full[:, :qkv_cols].reshape(model_width, 3, -1)
    proj_full = attn_full[:, qkv_cols:]
    gain_one, bias_one, proj_shift, gain_two, bias_two = (small_full[:, k] for k in range(5))
    router_full = small_full[:, 5 : 5 + experts]
    back_shift = small_full[:, 5 + experts : 5 + 2 * experts].T

    def scores_of(query_heads, key_heads):
        return (
            jnp.einsum(
                "bqhe,bkhe->bhqk", query_heads, key_heads, preferred_element_type=jnp.float32
            )
            * score_scale
        )

    gain_one_f = gain_one.astype(jnp.float32)
    bias_one_f = bias_one.astype(jnp.float32)
    source = inputs.astype(jnp.float32)
    rows_one = layer_norm(
        both_rows[:, 0].astype(jnp.float32), gain_one_f, bias_one_f
    ).astype(jnp.bfloat16)
    mixed = jnp.einsum(
        "bsd,dkf->bskf", rows_one, qkv_full, preferred_element_type=jnp.float32
    ).astype(jnp.bfloat16)
    head_blocks = mixed.reshape(group_images, seq_len, 3, heads_local, HEAD_DIM)
    query_heads = head_blocks[:, :, 0]
    key_heads = head_blocks[:, :, 1]
    value_heads = head_blocks[:, :, 2]
    scores = scores_of(query_heads, key_heads)
    top_score = jnp.max(scores, axis=-1, keepdims=True)
    raised = jnp.exp(scores - top_score)
    row_total = jnp.sum(raised, axis=-1, keepdims=True)
    weights = raised / row_total
    log_total = top_score + jnp.log(row_total)
    attended = jnp.einsum(
        "bhqk,bkhe->bqhe",
        weights.astype(jnp.bfloat16),
        value_heads,
        preferred_element_type=jnp.float32,
    )
    attended = attended.astype(jnp.bfloat16).reshape(group_images, seq_len, heads_local * HEAD_DIM)
    attn_terms = jnp.einsum("bsf,df->bsd", attended, proj_full, preferred_element_type=jnp.float32)
    attn_sum = scatter_rows(attn_terms)
    state = source + attn_sum + proj_shift.astype(jnp.float32)
    gain_two_f = gain_two.astype(jnp.float32)
    bias_two_f = bias_two.astype(jnp.float32)
    normed_two = layer_norm(state, gain_two_f, bias_two_f).astype(jnp.bfloat16)
    rows_two = lax.all_gather(normed_two, "tensor", axis=0, tiled=True)
    out_rows = both_rows[:, 1]
    token_rows = rows_two.reshape(tokens, model_width)
    grad_rows = out_rows.reshape(tokens, model_width)
    choice_ids = expert_ids.reshape(tokens, 2)
    places = choice_ids * slot_rows + slot_ids.reshape(tokens, 2)
    slot_index = jnp.arange(experts * slot_rows, dtype=jnp.int32)[:, None]
    chosen = (
        (slot_index == places[:, 0][None, :]) | (slot_index == places[:, 1][None, :])
    ).astype(jnp.bfloat16)
    logits = jnp.dot(token_rows, router_full, preferred_element_type=jnp.float32)
    router_probs = jax.nn.softmax(logits, axis=-1)
    expert_mask = (
        jnp.arange(experts * slot_rows)[:, None] // slot_rows == jnp.arange(experts)[None, :]
    )
    slot_probs = jnp.dot(chosen, split_three(router_probs), preferred_element_type=jnp.float32)
    slot_gates = jnp.sum(
        jnp.where(expert_mask[:, None, :], slot_probs.reshape(-1, 3, experts), 0.0), axis=(1, 2)
    )
    dispatched = (
        jnp.dot(chosen, token_rows, preferred_element_type=jnp.float32)
        .astype(jnp.bfloat16)
        .reshape(experts, slot_rows, model_width)
    )
    slot_out = (
        jnp.dot(chosen, grad_rows, preferred_element_type=jnp.float32)
    )
    slot_grad = (
        (slot_gates[:, None] * slot_out)
        .astype(jnp.bfloat16)
        .reshape(experts, slot_rows, model_width)
    )
    pre = (
        jnp.einsum("ecd,edf->ecf", dispatched, in_full, preferred_element_type=jnp.float32)
        + expert_in_bias.astype(jnp.float32)[:, None, :]
    )
    hidden = gelu_tanh(pre).astype(jnp.bfloat16)
    expert_terms = jnp.einsum(
        "ecf,edf->ecd", hidden, out_full, preferred_element_type=jnp.float32
    ).reshape(experts * slot_rows, model_width)
    gated_terms = (slot_gates[:, None] * expert_terms).astype(jnp.bfloat16)
    slot_dgate = jnp.sum(expert_terms * slot_out, axis=-1)
    mixed_terms = jnp.einsum(
        "st,sd->td", chosen, gated_terms, preferred_element_type=jnp.float32
    )
    mixed_sum = scatter_rows(mixed_terms.reshape(group_images, seq_len, model_width))
    own_ids = own_rows(expert_ids.reshape(group_images, seq_len, 2))
    onehot_own = (own_ids[..., None] == jnp.arange(experts)).astype(jnp.float32)
    probs_own = own_rows(router_probs.reshape(group_images, seq_len, experts))
    probs_chosen = probs_own * jnp.sum(onehot_own, axis=2)
    back_f = back_shift.astype(jnp.float32)
    shift_own = jnp.einsum("bpe,ed->bpd", probs_chosen, back_f, precision=PRECISE)
    result = state + mixed_sum + shift_own
    block_out = result.astype(jnp.bfloat16)
    own_grad = cotangent.astype(jnp.float32)
    out_grad = jnp.einsum("ecf,ecd->edf", hidden, slot_grad, preferred_element_type=jnp.float32)
    hidden_grad = jnp.einsum(
        "ecd,edf->ecf", slot_grad, out_full, preferred_element_type=jnp.float32
    )
    gelu_pull = jax.vjp(gelu_tanh, pre)[1]
    pre_grad = gelu_pull(hidden_grad)[0].astype(jnp.bfloat16)
    in_grad = jnp.einsum("ecd,ecf->edf", dispatched, pre_grad, preferred_element_type=jnp.float32)
    in_bias_grad = jnp.sum(pre_grad.astype(jnp.float32), axis=1)
    slot_back = (
        jnp.einsum("ecf,edf->ecd", pre_grad, in_full, preferred_element_type=jnp.float32)
        .astype(jnp.bfloat16)
        .reshape(experts * slot_rows, model_width)
    )
    row_back = jnp.einsum("st,sd->td", chosen, slot_back, preferred_element_type=jnp.float32)
    dgate_cols = split_three(jnp.where(expert_mask, slot_dgate[:, None], 0.0))
    prob_parts = jnp.sum(
        jnp.einsum("st,sk->tk", chosen, dgate_cols, preferred_element_type=jnp.float32).reshape(
            tokens, 3, experts
        ),
        axis=1,
    )
    row_sum = scatter_rows(row_back.reshape(group_images, seq_len, model_width))
    prob_sum = lax.psum_scatter(
        prob_parts.reshape(group_images, seq_len, experts),
        "tensor",
        scatter_dimension=0,
        tiled=True,
    )
    prob_grad = prob_sum + jnp.sum(onehot_own, axis=2) * jnp.einsum(
        "bpd,ed->bpe", own_grad, back_f, precision=PRECISE
    )
    logit_grad = probs_own * (prob_grad - jnp.sum(probs_own * prob_grad, axis=-1, keepdims=True))
    normed_grad = row_sum + jnp.einsum(
        "bpe,de->bpd", logit_grad, router_full.astype(jnp.float32), precision=PRECISE
    )
    router_grad = jnp.einsum(
        "bpd,bpe->de", normed_two.astype(jnp.float32), logit_grad, precision=PRECISE
    )
    back_bias_grad = jnp.einsum("bpe,bpd->ed", probs_chosen, own_grad, precision=PRECISE)
    norm_two_pull = jax.vjp(layer_norm, state, gain_two_f, bias_two_f)[1]
    state_grad, gain_two_grad, bias_two_grad = norm_two_pull(normed_grad)
    state_grad = state_grad + own_grad
    proj_bias_grad = jnp.sum(state_grad, axis=(0, 1))
    state_rows = lax.all_gather(state_grad.astype(jnp.bfloat16), "tensor", axis=0, tiled=True)
    proj_grad = jnp.einsum("bsf,bsd->df", attended, state_rows, preferred_element_type=jnp.float32)
    attended_grad = jnp.einsum(
        "bsd,df->bsf", state_rows, proj_full, preferred_element_type=jnp.float32
    )
    attended_grad = attended_grad.astype(jnp.bfloat16).reshape(
        group_images, seq_len, heads_local, HEAD_DIM
    )
    weight_grad = jnp.einsum(
        "bqhe,bkhe->bhqk", attended_grad, value_heads, preferred_element_type=jnp.float32
    )
    centre = jnp.sum(weights * weight_grad, axis=-1, keepdims=True)
    score_grad = (weights * (weight_grad - centre)).astype(jnp.bfloat16)
    query_grad = (
        jnp.einsum("bhqk,bkhe->bqhe", score_grad, key_heads, preferred_element_type=jnp.float32)
        * score_scale
    )
    key_grad = (
        jnp.einsum("bhqk,bqhe->bkhe", score_grad, query_heads, preferred_element_type=jnp.float32)
        * score_scale
    )
    value_grad = jnp.einsum(
        "bhqk,bqhe->bkhe",
        weights.astype(jnp.bfloat16),
        attended_grad,
        preferred_element_type=jnp.float32,
    )
    heads_grad = jnp.stack([query_grad, key_grad, value_grad], axis=2).astype(jnp.bfloat16)
    heads_grad = heads_grad.reshape(group_images, seq_len, 3, heads_local * HEAD_DIM)
    qkv_grad = jnp.einsum("bsd,bskf->dkf", rows_one, heads_grad, preferred_element_type=jnp.float32)
    rows_grad = jnp.einsum(
        "bskf,dkf->bsd", heads_grad, qkv_full, preferred_element_type=jnp.float32
    )
    normed_one_grad = scatter_rows(rows_grad)
    norm_one_pull = jax.vjp(layer_norm, source, gain_one_f, bias_one_f)[1]
    source_grad, gain_one_grad, bias_one_grad = norm_one_pull(normed_one_grad)
    input_grad = state_grad + source_grad
    hidden_cols = in_bias_grad.shape[1]
    bias_share = hidden_cols // dp_count
    attn_grad = jnp.concatenate(
        [qkv_grad.reshape(model_width, qkv_cols), proj_grad], axis=1
    )
    small_grad = jnp.concatenate(
        [
            jnp.stack(
                [gain_one_grad, bias_one_grad, proj_bias_grad, gain_two_grad, bias_two_grad],
                axis=1,
            ),
            router_grad,
            back_bias_grad.T,
            in_bias_grad.T,
        ],
        axis=1,
    )
    small_grad = jnp.pad(small_grad, ((0, 0), (0, 128 - small_grad.shape[1])))

    def blocks(values):
        return values.astype(jnp.bfloat16).reshape(
            -1, dp_count, values.shape[-2] // dp_count, values.shape[-1]
        )

    grads = [blocks(values) for values in (small_grad, attn_grad, in_grad, out_grad)]
    if by_kernel:
        small_part, attn_part, in_part, out_part = reduce_grads(*grads)
    else:
        small_part, attn_part, in_part, out_part = (
            lax.psum_scatter(values, "dp", scatter_dimension=1).astype(jnp.float32)
            for values in grads
        )
    small_part = small_part[0]
    norm_cols = 5 + 2 * experts
    totals = lax.psum(small_part[:, :norm_cols], "tensor")
    moves = []
    for source_dp in range(dp_count):
        for source_tensor in range(tensor_count):
            moves.append(
                (source_dp * tensor_count + source_tensor, source_tensor * dp_count + source_dp)
            )
    in_bias_out = lax.ppermute(
        small_part[:, norm_cols : norm_cols + experts].T, ("dp", "tensor"), moves
    )
    attn_part = attn_part[0]
    return (
        block_out,
        input_grad,
        totals[:, 0],
        totals[:, 1],
        attn_part[:, :qkv_cols].reshape(share, 3, -1),
        attn_part[:, qkv_cols:].T,
        totals[:, 2],
        totals[:, 3],
        totals[:, 4],
        totals[:, 5 : 5 + experts],
        in_part,
        in_bias_out,
        jnp.swapaxes(out_part, 1, 2),
        totals[:, 5 + experts : norm_cols].T,
    )


def solution(mesh):
    placed = (
        P(("dp", "tensor"), None, None),
        P("dp"),
        P("dp"),
        P("dp", None, "tensor"),
        P("tensor", "dp"),
        P("dp"),
        P("dp"),
        P("dp"),
        P("dp", None),
        P(None, "dp", "tensor"),
        P(None, "tensor"),
        P(None, "tensor", "dp"),
        P(None, "dp"),
        P("dp", None, None),
        P("dp", None, None),
        P(("dp", "tensor"), None, None),
    )
    return jax.shard_map(
        per_device,
        mesh=mesh,
        in_specs=placed,
        out_specs=(
            P(("dp", "tensor"), None, None),
            P(("dp", "tensor"), None, None),
            P("dp"),
            P("dp"),
            P("dp", None, "tensor"),
            P("tensor", "dp"),
            P("dp"),
            P("dp"),
            P("dp"),
            P("dp", None),
            P(None, "dp", "tensor"),
            P(None, ("dp", "tensor")),
            P(None, "tensor", "dp"),
            P(None, "dp"),
        ),
        check_vma=False,
    )
```
